256 devices in a mesh: gx: 4 (over y), gy: 16 (over z, core), gz: 4 (over x).
Axes of the slice: x: 4, y: 4, z: 8, core: 2. Of those that a mesh axis runs over, the one named last changes fastest.
Arguments:
- orbitals: float32 [4, 128, 256, 512], P(None, 'gz', 'gy', 'gx'), may hold values from -20 to 20
- potential: float32 [128, 256, 512], P('gz', 'gy', 'gx'), may hold values from -1.5 to 1.5
Outputs:
- orthonormal: float32 [4, 128, 256, 512], P(None, 'gz', 'gy', 'gx')
- factor: float32 [4, 4], replicated
The draws below stay inside these ranges and needn't reach their ends.
All inputs are finite; a program needn't handle non-finite values.
Results may differ from the reference program's by a relative error of at most 0.0003.
Values sent between devices are 32-bit elements; how exact they have to be, the bound alone decides.
A program may use at most 128 MiB of HBM per device.

```python
import math
import jax
import jax.numpy as jnp
from jax import lax

NORB = 4
DEG = 3
NX = 512
NY = 256
NZ = 128
NCELLS = 16777216


def alternating(length):
    index = jnp.arange(length, dtype=jnp.int32)
    return (1 - 2 * (index % 2)).astype(jnp.float32)


def draw_orbitals(key, part):
    key = jax.random.fold_in(key, 11)
    key_common = jax.random.fold_in(key, 1)
    key_own = jax.random.fold_in(key, 2)
    key_mix = jax.random.fold_in(key, 3)
    key_phase = jax.random.fold_in(key, 4)
    common = jax.random.truncated_normal(key_common, -4.0, 4.0, (NZ, NY, NX), jnp.float32)
    own = jax.random.truncated_normal(key_own, -4.0, 4.0, (NORB, NZ, NY, NX), jnp.float32)
    base = 3.0
    mixing = jax.random.uniform(key_mix, (NORB, 1, 1, 1), jnp.float32, -0.8, 0.8)
    phases = jax.random.uniform(key_phase, (NORB, 4), jnp.float32, 0.0, 2.0 * math.pi)
    lattice_index_east = jnp.arange(NX, dtype=jnp.float32)[None, None, :]
    lattice_index_north = jnp.arange(NY, dtype=jnp.float32)[None, :, None]
    lattice_index_upward = jnp.arange(NZ, dtype=jnp.float32)[:, None, None]
    evenness_east = alternating(NX)[None, None, :]
    evenness_north = alternating(NY)[None, :, None]
    evenness_upward = alternating(NZ)[:, None, None]
    plus_minus_layouts = []
    for orbit in range(NORB):
        kind_index = orbit % 4
        initial_angle = phases[orbit, 0]
        later_angle = phases[orbit, 1]
        if kind_index == 0:
            oscillating_factor = evenness_east * evenness_north * jnp.cos(1.42 * lattice_index_upward + initial_angle)
        elif kind_index == 1:
            oscillating_factor = evenness_north * evenness_upward * jnp.cos(1.42 * lattice_index_east + initial_angle)
        elif kind_index == 2:
            oscillating_factor = evenness_east * evenness_upward * jnp.cos(1.42 * lattice_index_north + initial_angle)
        else:
            oscillating_factor = evenness_east * jnp.cos(2.12 * lattice_index_north + initial_angle) * jnp.cos(2.12 * lattice_index_upward + later_angle)
        gentle_profile = 1.0 + 0.3 * jnp.cos(2.0 * math.pi * lattice_index_east / NX + phases[orbit, 2]) + 0.2 * jnp.cos(2.0 * math.pi * lattice_index_north / NY + phases[orbit, 3])
        plus_minus_layouts.append(oscillating_factor * gentle_profile)
    pattern = jnp.stack(plus_minus_layouts)
    ramp = 0.5 * lattice_index_east / NX + 0.3 * lattice_index_north / NY + 0.2 * lattice_index_upward / NZ
    rising = jnp.power(base, ramp)
    noise = 0.05 * (own + mixing * common[None])
    return (pattern + noise) * rising[None]


def block_scale(rng, extent, shards, low, high):
    factor_of, own = 1.0, jax.random.fold_in(rng, 6)
    for position, blocks in shards:
        draws = jnp.exp(jax.random.uniform(jax.random.fold_in(own, position), (blocks,), jnp.float32, low / len(shards), high / len(shards)))
        factor_of = factor_of * jnp.repeat(draws, extent[position] // blocks).reshape([-1 if axis == position else 1 for axis in range(len(extent))])
    return factor_of


def setup_inputs(seed: int = 0) -> dict:
    arg_keys = jax.random.split(jax.random.key(seed), 3)
    return {
        "orbitals": draw_orbitals(jax.random.fold_in(arg_keys[2], 71), 0),
        "potential": jnp.clip(jax.random.uniform(arg_keys[1], (NZ, NY, NX), jnp.float32, -1.5, 1.5) * block_scale(arg_keys[1], (NZ, NY, NX), ((0, 4), (1, 16), (2, 4)), -0.4, 0.0), -1.5, 1.5),
    }


stencil_weights = (-205.0 / 72.0, 8.0 / 5.0, -1.0 / 5.0, 8.0 / 315.0, -1.0 / 560.0)
lower_end = -1.5
cutoff = 3.0
upper_end = 12.0
half_width = (upper_end - cutoff) / 2.0
centre = (upper_end + cutoff) / 2.0
sigma_first = half_width / (lower_end - centre)

def apply_hamil(field, potential):
    laplace = 3.0 * stencil_weights[0] * field
    for shift in range(1, 5):
        beside_all = jnp.roll(field, shift, 0) + jnp.roll(field, -shift, 0)
        beside_all = beside_all + jnp.roll(field, shift, 1) + jnp.roll(field, -shift, 1)
        beside_all = beside_all + jnp.roll(field, shift, 2) + jnp.roll(field, -shift, 2)
        laplace = laplace + stencil_weights[shift] * beside_all
    return -0.5 * laplace + potential * field

def upper_inverse(upper):
    size_n = upper.shape[0]
    rows = [None] * size_n
    for i in reversed(range(size_n)):
        total = jnp.zeros((size_n,), jnp.float32).at[i].set(1.0)
        for j in range(i + 1, size_n):
            total = total - upper[i, j] * rows[j]
        rows[i] = total / upper[i, i]
    return jnp.stack(rows)

def reference(orbitals, potential):

    def filter_one(field):
        previous = field
        current = sigma_first / half_width * (apply_hamil(field, potential) - centre * field)
        sigma = sigma_first
        for step in range(DEG - 1):
            sigma_new = 1.0 / (2.0 / sigma_first - sigma)
            fresh = 2.0 * sigma_new / half_width * (apply_hamil(current, potential) - centre * current) - sigma * sigma_new * previous
            previous = current
            current = fresh
            sigma = sigma_new
        return current
    filtered = lax.map(filter_one, orbitals)
    gram = jnp.einsum('aijk,bijk->ab', filtered, filtered, precision=lax.Precision.HIGHEST) / float(NCELLS)
    factor = jnp.linalg.cholesky(gram).T
    inverse = upper_inverse(factor)
    orthonormal = jnp.einsum('aijk,ab->bijk', filtered, inverse, precision=lax.Precision.HIGHEST)
    return (orthonormal, factor)
```

```python
import functools

import jax
import jax.numpy as jnp
from jax import lax
from jax.experimental import pallas as pl
from jax.experimental.pallas import tpu as pltpu
from jax.sharding import PartitionSpec as P

DEG = 3
REACH = 4
LANES = 128
ROWS = 8
MESH = pl.DeviceIdType.MESH

stencil_weights = (-205.0 / 72.0, 8.0 / 5.0, -1.0 / 5.0, 8.0 / 315.0, -1.0 / 560.0)
lower_end = -1.5
cutoff = 3.0
upper_end = 12.0
half_width = (upper_end - cutoff) / 2.0
centre = (upper_end + cutoff) / 2.0
sigma_first = half_width / (lower_end - centre)


def recurrence():
    steps = [(sigma_first / half_width, 0.0)]
    sigma = sigma_first
    for _ in range(DEG - 1):
        sigma_new = 1.0 / (2.0 / sigma_first - sigma)
        steps.append((2.0 * sigma_new / half_width, sigma * sigma_new))
        sigma = sigma_new
    return steps


def edge_matrices():
    scaled = [round(5040.0 * weight) for weight in stencil_weights]
    row = lax.broadcasted_iota(jnp.int32, (2 * LANES, LANES), 0)
    col = lax.broadcasted_iota(jnp.int32, (2 * LANES, LANES), 1)
    part = row % ROWS
    edge = jnp.where(part < REACH, part - REACH, LANES - REACH + part)
    apart = jnp.abs(jnp.where(row < LANES, row, edge) - col)
    matrix = jnp.zeros((2 * LANES, LANES), jnp.float32)
    for k in range(1, REACH + 1):
        matrix = jnp.where(apart == k, float(scaled[k]), matrix)
    return matrix.astype(jnp.bfloat16)


def place_mask(vectors):
    row = lax.broadcasted_iota(jnp.int32, (vectors * ROWS, LANES), 0)
    col = lax.broadcasted_iota(jnp.int32, (vectors * ROWS, LANES), 1)
    return jnp.where(row // ROWS == col // ROWS, 1.0, 0.0).astype(jnp.bfloat16)


def thirds(value):
    first = value.astype(jnp.bfloat16)
    rest = value - first.astype(jnp.float32)
    second = rest.astype(jnp.bfloat16)
    third = (rest - second.astype(jnp.float32)).astype(jnp.bfloat16)
    return first, second, third


def filter_kernel(
    sizes,
    orbitals,
    potential,
    filtered,
    gram,
    field,
    raw,
    base,
    diagonal,
    x_send,
    x_recv,
    matrix,
    mask,
    partial,
    sums,
    load_sem,
    send_sem,
    recv_sem,
    gram_send_sem,
    gram_recv_sem,
    near_sem,
    line_sem,
    plane_sem,
):
    count_x, count_y, count_z = sizes
    norb, size_z, size_y = orbitals.shape[:3]
    groups = size_z // ROWS
    tiles = size_y // ROWS
    me_x, me_y, me_z = (lax.axis_index(a) for a in ("gx", "gy", "gz"))

    def at(dx, dy, dz):
        return (
            lax.rem(me_x + dx, count_x),
            lax.rem(me_y + dy, count_y),
            lax.rem(me_z + dz, count_z),
        )

    def greet(sem, offsets):
        for there in offsets:
            pl.semaphore_signal(sem, inc=1, device_id=at(*there), device_id_type=MESH)

    beside = [
        (1, 0, 0),
        (count_x - 1, 0, 0),
        (0, 1, 0),
        (0, count_y - 1, 0),
        (0, 0, 1),
        (0, 0, count_z - 1),
    ]
    near = [(2, 0, 0), (0, 2, 0), (0, count_y - 2, 0), (0, 0, 2)]
    line = [(0, 4, 0), (0, count_y - 4, 0)]
    plane = [(dx, 0, dz) for dx in range(count_x) for dz in range(count_z)][1:]

    barrier = pltpu.get_barrier_semaphore()
    greet(barrier, beside)

    body_z = pl.ds(REACH, size_z)
    body_y = pl.ds(ROWS, size_y)

    loads = [
        pltpu.make_async_copy(
            orbitals.at[o], field.at[0, o, body_z, body_y], load_sem.at[o]
        )
        for o in range(norb)
    ]
    loads.append(pltpu.make_async_copy(potential, raw, load_sem.at[norb]))
    for load in loads:
        load.start()

    lane = lax.broadcasted_iota(jnp.int32, (ROWS, LANES), 1)
    matrix[...] = edge_matrices()
    mask[...] = place_mask(ROWS * tiles)
    partial[...] = jnp.zeros_like(partial)

    def face_copies(step, o):
        def remote(src, dst, kind, there):
            return pltpu.make_async_remote_copy(
                src_ref=src,
                dst_ref=dst,
                send_sem=send_sem.at[step, o, kind],
                recv_sem=recv_sem.at[step, o, kind],
                device_id=at(*there),
                device_id_type=MESH,
            )

        def layers(first):
            return field.at[step, o, pl.ds(first, REACH), body_y]

        def rows(first):
            return field.at[step, o, body_z, pl.ds(first, REACH)]

        return [
            remote(rows(ROWS), rows(ROWS + size_y), 0, (0, count_y - 1, 0)),
            remote(rows(ROWS + size_y - REACH), rows(ROWS - REACH), 0, (0, 1, 0)),
            remote(layers(REACH), layers(REACH + size_z), 1, (0, 0, count_z - 1)),
            remote(layers(size_z), layers(0), 1, (0, 0, 1)),
            remote(x_send.at[step, o], x_recv.at[step, o, 1], 2, (count_x - 1, 0, 0)),
            remote(x_send.at[step, o], x_recv.at[step, o, 0], 2, (1, 0, 0)),
        ]

    def send_faces(step, o):
        for copy in face_copies(step, o):
            copy.start()

    def wait_faces(sem, step, o):
        for kind, span in (
            (0, field.at[step, o, body_z, pl.ds(0, 2 * REACH)]),
            (1, field.at[step, o, pl.ds(0, 2 * REACH), body_y]),
            (2, x_recv.at[step, o]),
        ):
            pltpu.make_async_copy(span, span, sem.at[step, o, kind]).wait()

    def put_edges(place, value, packed):
        moved = pltpu.roll(value, (REACH + ROWS * place) % LANES, 1)
        return jnp.where(lane // ROWS == place, moved, packed)

    def pack(o):
        def group(g, _):
            packed = jnp.zeros((ROWS, LANES), jnp.float32)
            for zz in range(ROWS):
                for tile in range(tiles):
                    z = g * ROWS + zz
                    value = field[0, o, REACH + z, pl.ds(ROWS * (1 + tile), ROWS)]
                    packed = put_edges(zz * tiles + tile, value, packed)
            x_send[0, o, g] = packed
            return 0

        lax.fori_loop(0, groups, group, 0, unroll=2)

    for o in range(norb):
        loads[o].wait()
        pack(o)
        if o == 0:
            pl.semaphore_wait(barrier, len(beside))
        send_faces(0, o)

    loads[norb].wait()
    steps = recurrence()

    def settle(z, _):
        level = raw[z] + (-1.5 * stencil_weights[0] - centre)
        for step, (alpha, _) in enumerate(steps):
            diagonal[step, z] = alpha * level
        return 0

    lax.fori_loop(0, size_z, settle, 0, unroll=4)

    def weights_of(alpha):
        return [alpha * (-0.5 * weight) for weight in stencil_weights], alpha * (-0.5 / 5040.0)

    def prepare(step, o, alpha, gamma):
        weights, from_scaled = weights_of(alpha)
        for g in range(groups):
            inside = field[step, o, pl.ds(REACH + ROWS * g, ROWS), body_y].reshape(-1, LANES)
            along_x = None
            for cells in thirds(inside):
                term = jnp.dot(cells, matrix[:LANES], preferred_element_type=jnp.float32)
                along_x = term if along_x is None else along_x + term
            along_x = along_x.reshape(ROWS, tiles, ROWS, LANES)
            for tile in range(tiles):
                first = ROWS * (1 + tile)
                inward = 1 - 2 * tile
                planes = {
                    z: field[step, o, REACH + z, pl.ds(first, ROWS)]
                    for z in range(ROWS * g - REACH, ROWS * (g + 1) + REACH)
                    if 0 <= z < size_z
                }
                for zz in range(ROWS):
                    z = ROWS * g + zz
                    total = diagonal[step, z, pl.ds(ROWS * tile, ROWS)] * planes[z]
                    total += from_scaled * along_x[zz, tile]
                    for k in range(1, REACH + 1):
                        around = field[step, o, REACH + z, pl.ds(first + inward * k, ROWS)]
                        for other in (z - k, z + k):
                            if other in planes:
                                around += planes[other]
                        total += weights[k] * around
                    if gamma is not None:
                        total -= gamma * field[step - 1, o, REACH + z, pl.ds(first, ROWS)]
                    base[o, z, pl.ds(ROWS * tile, ROWS)] = total

    def finish(step, o, alpha, last):
        weights, from_scaled = weights_of(alpha)
        for g in range(groups):
            edges = jnp.where(
                lane % ROWS < REACH, x_recv[step, o, 0, g], x_recv[step, o, 1, g]
            )
            ends = [
                jnp.concatenate([part] * (ROWS * tiles), 0) * mask[...] for part in thirds(edges)
            ]
            outside = matrix[LANES:]
            along_x = jnp.dot(
                jnp.concatenate(ends[:2], 1),
                jnp.concatenate([outside, outside], 0),
                preferred_element_type=jnp.float32,
            ) + jnp.dot(ends[2], outside, preferred_element_type=jnp.float32)
            along_x = along_x.reshape(ROWS, tiles, ROWS, LANES)
            packed = jnp.zeros((ROWS, LANES), jnp.float32)
            for tile in range(tiles):
                first = ROWS * (1 + tile)
                outward = 2 * tile - 1
                for zz in range(ROWS):
                    z = ROWS * g + zz
                    total = base[o, z, pl.ds(ROWS * tile, ROWS)] + from_scaled * along_x[zz, tile]
                    for k in range(1, REACH + 1):
                        around = field[step, o, REACH + z, pl.ds(first + outward * k, ROWS)]
                        for other in (z - k, z + k):
                            if not 0 <= other < size_z:
                                around += field[step, o, REACH + other, pl.ds(first, ROWS)]
                        total += weights[k] * around
                    if last:
                        filtered[o, z, pl.ds(ROWS * tile, ROWS)] = total
                    else:
                        field[step + 1, o, REACH + z, pl.ds(first, ROWS)] = total
                        packed = put_edges(zz * tiles + tile, total, packed)
            if not last:
                x_send[step + 1, o, g] = packed

    def begin(o, _):
        prepare(0, o, steps[0][0], None)
        return 0

    lax.fori_loop(0, norb, begin, 0)

    def early(q, _):
        step, o = q // norb, lax.rem(q, norb)
        wait_faces(recv_sem, step, o)

        @pl.when(q == 0)
        def _():
            greet(near_sem, near)

        finish(step, o, jnp.where(step == 0, steps[0][0], steps[1][0]), False)
        send_faces(step + 1, o)
        alpha, gamma = (
            jnp.where(step == 0, first, second) for first, second in zip(steps[1], steps[2])
        )
        prepare(step + 1, o, alpha, gamma)

        @pl.when(q == norb - 1)
        def _():
            pl.semaphore_wait(near_sem, len(near))
            greet(line_sem, line)

        @pl.when(q == (DEG - 1) * norb - 1)
        def _():
            pl.semaphore_wait(line_sem, len(line))
            greet(plane_sem, plane)

        return 0

    lax.fori_loop(0, (DEG - 1) * norb, early, 0)

    def gram_row(o):
        def add(z, totals):
            for tile in range(tiles):
                rows = pl.ds(ROWS * tile, ROWS)
                mine = filtered[o, z, rows]
                totals = tuple(
                    totals[b] + mine * (mine if b == o else filtered[b, z, rows])
                    for b in range(o + 1)
                )
            return totals

        start = (jnp.zeros((ROWS, LANES), jnp.float32),) * (o + 1)
        totals = lax.fori_loop(0, size_z, add, start, unroll=8)
        for b in range(o + 1):
            partial[o * norb + b] = totals[b]

    def late(o, _):
        wait_faces(recv_sem, DEG - 1, o)
        finish(DEG - 1, o, steps[DEG - 1][0], True)
        for k in range(norb):
            pl.when(o == k)(functools.partial(gram_row, k))
        return 0

    lax.fori_loop(0, norb, late, 0)

    own = jnp.zeros((ROWS, LANES), jnp.float32)
    for a in range(norb):
        for b in range(a + 1):
            pair = a * norb + b
            own = jnp.where(lane == pair, jnp.sum(partial[pair], axis=1, keepdims=True), own)
    slot = (me_x * count_y + me_y) * count_z + me_z
    sums[slot] = jnp.sum(own, axis=0, keepdims=True)

    pl.semaphore_wait(plane_sem, len(plane))

    def share(dy, there):
        pltpu.make_async_remote_copy(
            src_ref=sums.at[slot],
            dst_ref=sums.at[slot],
            send_sem=gram_send_sem,
            recv_sem=gram_recv_sem,
            device_id=at(there[0], dy, there[1]),
            device_id_type=MESH,
        ).start()

    by_plane = sorted(
        ((dx, dz) for dx in range(count_x) for dz in range(count_z)),
        key=lambda d: -min(d[0], count_x - d[0]) - min(d[1], count_z - d[1]),
    )

    def far_line(i, _):
        dy = count_y // 2 + (1 - 2 * lax.rem(i, 2)) * ((i + 1) // 2)
        for there in by_plane:
            share(dy, there)
        return 0

    lax.fori_loop(0, count_y - 1, far_line, 0)
    for there in by_plane[:-1]:
        share(0, there)

    def drain(i, _):
        wait_faces(send_sem, i // norb, lax.rem(i, norb))
        return 0

    lax.fori_loop(0, DEG * norb, drain, 0)

    devices = count_x * count_y * count_z
    others = sums.at[pl.ds(0, devices - 1)]
    pltpu.make_async_copy(others, others, gram_recv_sem).wait()

    width = 16

    def add_up(i, total):
        return total + sums[pl.ds(pl.multiple_of(i * width, width), width)]

    total = lax.fori_loop(1, devices // width, add_up, sums[pl.ds(0, width)], unroll=5)
    while total.shape[0] > 1:
        half = total.shape[0] // 2
        total = total[:half] + total[half:]
    gram[...] = total[0]
    pltpu.make_async_copy(others, others, gram_send_sem).wait()


def combine_kernel(ncells, gram, filtered, result, factor, out, store_sem):
    norb, size_z, size_y = filtered.shape[:3]
    lane = lax.broadcasted_iota(jnp.int32, (ROWS, LANES), 1)
    sums = jnp.broadcast_to(gram[...], (ROWS, LANES))

    def entry(a, b):
        pair = max(a, b) * norb + min(a, b)
        value = jnp.sum(jnp.where(lane == pair, sums, 0.0), axis=1, keepdims=True)
        return jnp.broadcast_to(value, (ROWS, LANES)) / ncells

    upper = [[None] * norb for _ in range(norb)]
    inverse = [[None] * norb for _ in range(norb)]
    for i in range(norb):
        for j in range(i, norb):
            rest = entry(i, j)
            for m in range(i):
                rest = rest - upper[m][i] * upper[m][j]
            if i == j:
                upper[i][i] = jnp.sqrt(rest)
                inverse[i][i] = 1.0 / upper[i][i]
            else:
                upper[i][j] = rest * inverse[i][i]
    for i in reversed(range(norb)):
        for j in range(i + 1, norb):
            rest = upper[i][i + 1] * inverse[i + 1][j]
            for m in range(i + 2, j + 1):
                rest = rest + upper[i][m] * inverse[m][j]
            inverse[i][j] = -rest * inverse[i][i]

    row = lax.broadcasted_iota(jnp.int32, (norb, norb), 0)
    col = lax.broadcasted_iota(jnp.int32, (norb, norb), 1)
    matrix = jnp.zeros((norb, norb), jnp.float32)
    for i in range(norb):
        for j in range(i, norb):
            matrix = jnp.where((row == i) & (col == j), upper[i][j][:norb, :norb], matrix)
    factor[...] = matrix

    chunks = store_sem.shape[0]
    length = size_z // chunks
    stores = []
    for c in range(chunks):

        def one(z, _):
            for tile in range(size_y // ROWS):
                rows = pl.ds(ROWS * tile, ROWS)
                held = [filtered[a, z, rows] for a in range(norb)]
                for b in range(norb):
                    total = held[0] * inverse[0][b]
                    for a in range(1, b + 1):
                        total = total + held[a] * inverse[a][b]
                    out[b, z, rows] = total
            return 0

        lax.fori_loop(c * length, (c + 1) * length, one, 0, unroll=4)
        part = pl.ds(c * length, length)
        stores.append(
            pltpu.make_async_copy(out.at[:, part], result.at[:, part], store_sem.at[c])
        )
        stores[-1].start()
    for store in stores:
        store.wait()


def per_device(sizes, ncells, orbitals, potential):
    norb, size_z, size_y, size_x = orbitals.shape
    assert size_x == LANES and size_z % ROWS == 0 and size_y == 2 * ROWS
    assert sizes == (4, 16, 4)
    hbm = pl.BlockSpec(memory_space=pltpu.HBM)
    vmem = pl.BlockSpec(memory_space=pltpu.VMEM)
    f32 = jnp.float32
    groups = size_z // ROWS
    devices = sizes[0] * sizes[1] * sizes[2]
    orbitals = pltpu.with_memory_space_constraint(orbitals, pltpu.HBM)
    potential = pltpu.with_memory_space_constraint(potential, pltpu.HBM)
    filtered, gram = pl.pallas_call(
        functools.partial(filter_kernel, sizes),
        out_shape=(
            jax.ShapeDtypeStruct(orbitals.shape, f32),
            jax.ShapeDtypeStruct((1, LANES), f32),
        ),
        in_specs=[hbm, hbm],
        out_specs=(vmem, vmem),
        scratch_shapes=[
            pltpu.VMEM((DEG, norb, size_z + 2 * REACH, size_y + 2 * ROWS, LANES), f32),
            pltpu.VMEM((size_z, size_y, LANES), f32),
            pltpu.VMEM(orbitals.shape, f32),
            pltpu.VMEM((DEG, size_z, size_y, LANES), f32),
            pltpu.VMEM((DEG, norb, groups, ROWS, LANES), f32),
            pltpu.VMEM((DEG, norb, 2, groups, ROWS, LANES), f32),
            pltpu.VMEM((2 * LANES, LANES), jnp.bfloat16),
            pltpu.VMEM((ROWS * size_y, LANES), jnp.bfloat16),
            pltpu.VMEM((norb * norb, ROWS, LANES), f32),
            pltpu.VMEM((devices, 1, LANES), f32),
            pltpu.SemaphoreType.DMA((norb + 1,)),
            pltpu.SemaphoreType.DMA((DEG, norb, 3)),
            pltpu.SemaphoreType.DMA((DEG, norb, 3)),
            pltpu.SemaphoreType.DMA,
            pltpu.SemaphoreType.DMA,
            pltpu.SemaphoreType.REGULAR,
            pltpu.SemaphoreType.REGULAR,
            pltpu.SemaphoreType.REGULAR,
        ],
        compiler_params=pltpu.CompilerParams(
            collective_id=0, has_side_effects=True, vmem_limit_bytes=32 * 2**20
        ),
        name="filter_and_gram",
    )(orbitals, potential)
    return pl.pallas_call(
        functools.partial(combine_kernel, ncells),
        out_shape=(
            jax.ShapeDtypeStruct(orbitals.shape, f32),
            jax.ShapeDtypeStruct((norb, norb), f32),
        ),
        in_specs=[vmem, vmem],
        out_specs=(hbm, vmem),
        scratch_shapes=[
            pltpu.VMEM(orbitals.shape, f32),
            pltpu.SemaphoreType.DMA((4,)),
        ],
        compiler_params=pltpu.CompilerParams(vmem_limit_bytes=16 * 2**20),
        name="combine",
    )(gram, filtered)


def solution(mesh):
    sizes = tuple(mesh.shape[a] for a in ("gx", "gy", "gz"))

    def run(orbitals, potential):
        ncells = float(potential.size)
        return jax.shard_map(
            functools.partial(per_device, sizes, ncells),
            mesh=mesh,
            in_specs=(P(None, "gz", "gy", "gx"), P("gz", "gy", "gx")),
            out_specs=(P(None, "gz", "gy", "gx"), P()),
            check_vma=False,
        )(orbitals, potential)

    return run
```

```python
import functools

import jax
import jax.numpy as jnp
from jax import lax
from jax.experimental import pallas as pl
from jax.experimental.pallas import tpu as pltpu
from jax.sharding import PartitionSpec as P

DEG = 3
REACH = 4
LANES = 128
ROWS = 8
MESH = pl.DeviceIdType.MESH

stencil_weights = (-205.0 / 72.0, 8.0 / 5.0, -1.0 / 5.0, 8.0 / 315.0, -1.0 / 560.0)
lower_end = -1.5
cutoff = 3.0
upper_end = 12.0
half_width = (upper_end - cutoff) / 2.0
centre = (upper_end + cutoff) / 2.0
sigma_first = half_width / (lower_end - centre)


def recurrence():
    steps = [(sigma_first / half_width, 0.0)]
    sigma = sigma_first
    for _ in range(DEG - 1):
        sigma_new = 1.0 / (2.0 / sigma_first - sigma)
        steps.append((2.0 * sigma_new / half_width, sigma * sigma_new))
        sigma = sigma_new
    return steps


def edge_matrices():
    scaled = [round(5040.0 * weight) for weight in stencil_weights]
    row = lax.broadcasted_iota(jnp.int32, (2 * LANES, LANES), 0)
    col = lax.broadcasted_iota(jnp.int32, (2 * LANES, LANES), 1)
    part = row % ROWS
    edge = jnp.where(part < REACH, part - REACH, LANES - REACH + part)
    apart = jnp.abs(jnp.where(row < LANES, row, edge) - col)
    matrix = jnp.zeros((2 * LANES, LANES), jnp.float32)
    for k in range(1, REACH + 1):
        matrix = jnp.where(apart == k, float(scaled[k]), matrix)
    return matrix.astype(jnp.bfloat16)


def place_mask(vectors):
    row = lax.broadcasted_iota(jnp.int32, (vectors * ROWS, LANES), 0)
    col = lax.broadcasted_iota(jnp.int32, (vectors * ROWS, LANES), 1)
    return jnp.where(row // ROWS == col // ROWS, 1.0, 0.0).astype(jnp.bfloat16)


def thirds(value):
    first = value.astype(jnp.bfloat16)
    rest = value - first.astype(jnp.float32)
    second = rest.astype(jnp.bfloat16)
    third = (rest - second.astype(jnp.float32)).astype(jnp.bfloat16)
    return first, second, third


def filter_kernel(
    sizes,
    orbitals,
    potential,
    filtered,
    gram,
    field,
    raw,
    base,
    diagonal,
    x_send,
    x_recv,
    matrix,
    mask,
    partial,
    sums,
    load_sem,
    send_sem,
    recv_sem,
    gram_send_sem,
    gram_recv_sem,
    near_sem,
    line_sem,
    plane_sem,
):
    count_x, count_y, count_z = sizes
    norb, size_z, size_y = orbitals.shape[:3]
    groups = size_z // ROWS
    tiles = size_y // ROWS
    me_x, me_y, me_z = (lax.axis_index(a) for a in ("gx", "gy", "gz"))

    def at(dx, dy, dz):
        return (
            lax.rem(me_x + dx, count_x),
            lax.rem(me_y + dy, count_y),
            lax.rem(me_z + dz, count_z),
        )

    def greet(sem, offsets):
        for there in offsets:
            pl.semaphore_signal(sem, inc=1, device_id=at(*there), device_id_type=MESH)

    beside = [
        (1, 0, 0),
        (count_x - 1, 0, 0),
        (0, 1, 0),
        (0, count_y - 1, 0),
        (0, 0, 1),
        (0, 0, count_z - 1),
    ]
    near = [(2, 0, 0), (0, 2, 0), (0, count_y - 2, 0), (0, 0, 2)]
    line = [(0, 4, 0), (0, count_y - 4, 0)]
    plane = [(dx, 0, dz) for dx in range(count_x) for dz in range(count_z)][1:]

    barrier = pltpu.get_barrier_semaphore()
    greet(barrier, beside)

    body_z = pl.ds(REACH, size_z)
    body_y = pl.ds(ROWS, size_y)

    loads = [
        pltpu.make_async_copy(
            orbitals.at[o], field.at[0, o, body_z, body_y], load_sem.at[o]
        )
        for o in range(norb)
    ]
    loads.append(pltpu.make_async_copy(potential, raw, load_sem.at[norb]))
    for load in loads:
        load.start()

    lane = lax.broadcasted_iota(jnp.int32, (ROWS, LANES), 1)
    matrix[...] = edge_matrices()
    mask[...] = place_mask(ROWS * tiles)
    partial[...] = jnp.zeros_like(partial)

    def face_copies(step, o):
        def remote(src, dst, kind, there):
            return pltpu.make_async_remote_copy(
                src_ref=src,
                dst_ref=dst,
                send_sem=send_sem.at[step, o, kind],
                recv_sem=recv_sem.at[step, o, kind],
                device_id=at(*there),
                device_id_type=MESH,
            )

        def layers(first):
            return field.at[step, o, pl.ds(first, REACH), body_y]

        def rows(first):
            return field.at[step, o, body_z, pl.ds(first, REACH)]

        return [
            remote(x_send.at[step, o], x_recv.at[step, o, 1], 2, (count_x - 1, 0, 0)),
            remote(x_send.at[step, o], x_recv.at[step, o, 0], 2, (1, 0, 0)),
            remote(layers(REACH), layers(REACH + size_z), 1, (0, 0, count_z - 1)),
            remote(layers(size_z), layers(0), 1, (0, 0, 1)),
            remote(rows(ROWS), rows(ROWS + size_y), 0, (0, count_y - 1, 0)),
            remote(rows(ROWS + size_y - REACH), rows(ROWS - REACH), 0, (0, 1, 0)),
        ]

    def send_faces(step, o):
        for copy in face_copies(step, o):
            copy.start()

    def wait_faces(sem, step, o):
        for kind, span in (
            (0, field.at[step, o, body_z, pl.ds(0, 2 * REACH)]),
            (1, field.at[step, o, pl.ds(0, 2 * REACH), body_y]),
            (2, x_recv.at[step, o]),
        ):
            pltpu.make_async_copy(span, span, sem.at[step, o, kind]).wait()

    def put_edges(place, value, packed):
        moved = pltpu.roll(value, (REACH + ROWS * place) % LANES, 1)
        return jnp.where(lane // ROWS == place, moved, packed)

    def pack(o):
        def group(g, _):
            packed = jnp.zeros((ROWS, LANES), jnp.float32)
            for zz in range(ROWS):
                for tile in range(tiles):
                    z = g * ROWS + zz
                    value = field[0, o, REACH + z, pl.ds(ROWS * (1 + tile), ROWS)]
                    packed = put_edges(zz * tiles + tile, value, packed)
            x_send[0, o, g] = packed
            return 0

        lax.fori_loop(0, groups, group, 0, unroll=2)

    for o in range(norb):
        loads[o].wait()
        pack(o)
        if o == 0:
            pl.semaphore_wait(barrier, len(beside))
        send_faces(0, o)

    loads[norb].wait()
    steps = recurrence()

    def settle(z, _):
        level = raw[z] + (-1.5 * stencil_weights[0] - centre)
        for step, (alpha, _) in enumerate(steps):
            diagonal[step, z] = alpha * level
        return 0

    lax.fori_loop(0, size_z, settle, 0, unroll=4)

    def weights_of(alpha):
        return [alpha * (-0.5 * weight) for weight in stencil_weights], alpha * (-0.5 / 5040.0)

    def prepare(step, o, alpha, gamma):
        weights, from_scaled = weights_of(alpha)
        for g in range(groups):
            inside = field[step, o, pl.ds(REACH + ROWS * g, ROWS), body_y].reshape(-1, LANES)
            along_x = None
            for cells in thirds(inside):
                term = jnp.dot(cells, matrix[:LANES], preferred_element_type=jnp.float32)
                along_x = term if along_x is None else along_x + term
            along_x = along_x.reshape(ROWS, tiles, ROWS, LANES)
            for tile in range(tiles):
                first = ROWS * (1 + tile)
                inward = 1 - 2 * tile
                planes = {
                    z: field[step, o, REACH + z, pl.ds(first, ROWS)]
                    for z in range(ROWS * g - REACH, ROWS * (g + 1) + REACH)
                    if 0 <= z < size_z
                }
                for zz in range(ROWS):
                    z = ROWS * g + zz
                    total = diagonal[step, z, pl.ds(ROWS * tile, ROWS)] * planes[z]
                    total += from_scaled * along_x[zz, tile]
                    for k in range(1, REACH + 1):
                        around = field[step, o, REACH + z, pl.ds(first + inward * k, ROWS)]
                        for other in (z - k, z + k):
                            if other in planes:
                                around += planes[other]
                        total += weights[k] * around
                    if gamma is not None:
                        total -= gamma * field[step - 1, o, REACH + z, pl.ds(first, ROWS)]
                    base[o, z, pl.ds(ROWS * tile, ROWS)] = total

    def finish(step, o, alpha, last):
        weights, from_scaled = weights_of(alpha)
        for g in range(groups):
            edges = jnp.where(
                lane % ROWS < REACH, x_recv[step, o, 0, g], x_recv[step, o, 1, g]
            )
            ends = [
                jnp.concatenate([part] * (ROWS * tiles), 0) * mask[...] for part in thirds(edges)
            ]
            outside = matrix[LANES:]
            along_x = jnp.dot(
                jnp.concatenate(ends[:2], 1),
                jnp.concatenate([outside, outside], 0),
                preferred_element_type=jnp.float32,
            ) + jnp.dot(ends[2], outside, preferred_element_type=jnp.float32)
            along_x = along_x.reshape(ROWS, tiles, ROWS, LANES)
            packed = jnp.zeros((ROWS, LANES), jnp.float32)
            for tile in range(tiles):
                first = ROWS * (1 + tile)
                outward = 2 * tile - 1
                for zz in range(ROWS):
                    z = ROWS * g + zz
                    total = base[o, z, pl.ds(ROWS * tile, ROWS)] + from_scaled * along_x[zz, tile]
                    for k in range(1, REACH + 1):
                        around = field[step, o, REACH + z, pl.ds(first + outward * k, ROWS)]
                        for other in (z - k, z + k):
                            if not 0 <= other < size_z:
                                around += field[step, o, REACH + other, pl.ds(first, ROWS)]
                        total += weights[k] * around
                    if last:
                        filtered[o, z, pl.ds(ROWS * tile, ROWS)] = total
                    else:
                        field[step + 1, o, REACH + z, pl.ds(first, ROWS)] = total
                        packed = put_edges(zz * tiles + tile, total, packed)
            if not last:
                x_send[step + 1, o, g] = packed

    def begin(o, _):
        prepare(0, o, steps[0][0], None)
        return 0

    lax.fori_loop(0, norb, begin, 0)

    def early(q, _):
        step, o = q // norb, lax.rem(q, norb)
        wait_faces(recv_sem, step, o)

        @pl.when(q == 0)
        def _():
            greet(near_sem, near)

        finish(step, o, jnp.where(step == 0, steps[0][0], steps[1][0]), False)
        send_faces(step + 1, o)
        alpha, gamma = (
            jnp.where(step == 0, first, second) for first, second in zip(steps[1], steps[2])
        )
        prepare(step + 1, o, alpha, gamma)

        @pl.when(q == norb - 1)
        def _():
            pl.semaphore_wait(near_sem, len(near))
            greet(line_sem, line)

        @pl.when(q == (DEG - 1) * norb - 1)
        def _():
            pl.semaphore_wait(line_sem, len(line))
            greet(plane_sem, plane)

        return 0

    lax.fori_loop(0, (DEG - 1) * norb, early, 0)

    def gram_row(o):
        def add(z, totals):
            fresh = []
            for tile in range(tiles):
                rows = pl.ds(ROWS * tile, ROWS)
                mine = filtered[o, z, rows]
                for b in range(o + 1):
                    other = mine if b == o else filtered[b, z, rows]
                    fresh.append(totals[len(fresh)] + mine * other)
            return tuple(fresh)

        start = (jnp.zeros((ROWS, LANES), jnp.float32),) * (tiles * (o + 1))
        totals = lax.fori_loop(0, size_z, add, start, unroll=16)
        for b in range(o + 1):
            partial[o * norb + b] = sum(totals[b + o + 1 :: o + 1], totals[b])

    def late(o, _):
        wait_faces(recv_sem, DEG - 1, o)
        finish(DEG - 1, o, steps[DEG - 1][0], True)
        for k in range(norb):
            pl.when(o == k)(functools.partial(gram_row, k))
        return 0

    lax.fori_loop(0, norb, late, 0)

    own = jnp.zeros((ROWS, LANES), jnp.float32)
    for a in range(norb):
        for b in range(a + 1):
            pair = a * norb + b
            own = jnp.where(lane == pair, jnp.sum(partial[pair], axis=1, keepdims=True), own)
    slot = (me_x * count_y + me_y) * count_z + me_z
    sums[pl.ds(slot, 1)] = jnp.sum(own, axis=0, keepdims=True)

    pl.semaphore_wait(plane_sem, len(plane))

    chips = count_y // 2
    chip, core = me_y // 2, lax.rem(me_y, 2)
    xs = [lax.rem(me_x + d, count_x) for d in range(count_x)]
    zs = [lax.rem(me_z + d, count_z) for d in range(count_z)]
    ys = []
    for d in range(chips):
        start = 2 * lax.rem(chip + d, chips)
        ys.append((start + core, start + 1 - core))

    def hops(there):
        return sum(min(d, n - d) for d, n in zip(there[:3], (count_x, chips, count_z)))

    everyone = [
        (dx, dc, dz, other)
        for dx in range(count_x)
        for dc in range(chips)
        for dz in range(count_z)
        for other in range(2)
    ]
    for dx, dc, dz, other in sorted(everyone[1:], key=hops, reverse=True):
        pltpu.make_async_remote_copy(
            src_ref=sums.at[pl.ds(slot, 1)],
            dst_ref=sums.at[pl.ds(slot, 1)],
            send_sem=gram_send_sem,
            recv_sem=gram_recv_sem,
            device_id=(xs[dx], ys[dc][other], zs[dz]),
            device_id_type=MESH,
        ).start()

    def drain(i, _):
        wait_faces(send_sem, i // norb, lax.rem(i, norb))
        return 0

    lax.fori_loop(0, DEG * norb, drain, 0)

    devices = count_x * count_y * count_z
    others = sums.at[pl.ds(0, devices - 1)]
    pltpu.make_async_copy(others, others, gram_recv_sem).wait()

    total = [sums[pl.ds(ROWS * i, ROWS)] for i in range(devices // ROWS)]
    while len(total) > 1:
        total = [one + two for one, two in zip(total[::2], total[1::2])]
    gram[...] = jnp.sum(total[0], axis=0, keepdims=True)
    pltpu.make_async_copy(others, others, gram_send_sem).wait()


def combine_kernel(ncells, gram, filtered, result, factor, out, upper_held, store_sem, factor_sem):
    norb, size_z, size_y = filtered.shape[:3]
    lane = lax.broadcasted_iota(jnp.int32, (ROWS, LANES), 1)
    sums = jnp.broadcast_to(gram[...], (ROWS, LANES))

    def entry(a, b):
        pair = max(a, b) * norb + min(a, b)
        value = jnp.sum(jnp.where(lane == pair, sums, 0.0), axis=1, keepdims=True)
        return jnp.broadcast_to(value, (ROWS, LANES)) / ncells

    upper = [[None] * norb for _ in range(norb)]
    inverse = [[None] * norb for _ in range(norb)]
    for i in range(norb):
        for j in range(i, norb):
            rest = entry(i, j)
            for m in range(i):
                rest = rest - upper[m][i] * upper[m][j]
            if i == j:
                upper[i][i] = jnp.sqrt(rest)
                inverse[i][i] = 1.0 / upper[i][i]
            else:
                upper[i][j] = rest * inverse[i][i]
    for i in reversed(range(norb)):
        for j in range(i + 1, norb):
            rest = upper[i][i + 1] * inverse[i + 1][j]
            for m in range(i + 2, j + 1):
                rest = rest + upper[i][m] * inverse[m][j]
            inverse[i][j] = -rest * inverse[i][i]

    row = lax.broadcasted_iota(jnp.int32, (norb, norb), 0)
    col = lax.broadcasted_iota(jnp.int32, (norb, norb), 1)
    matrix = jnp.zeros((norb, norb), jnp.float32)
    for i in range(norb):
        for j in range(i, norb):
            matrix = jnp.where((row == i) & (col == j), upper[i][j][:norb, :norb], matrix)
    upper_held[...] = matrix
    factor_store = pltpu.make_async_copy(upper_held, factor, factor_sem)
    factor_store.start()

    chunks = store_sem.shape[0]
    length = size_z // chunks
    stores = []
    for c in range(chunks):

        def one(z, _):
            for tile in range(size_y // ROWS):
                rows = pl.ds(ROWS * tile, ROWS)
                held = [filtered[a, z, rows] for a in range(norb)]
                for b in range(norb):
                    total = held[0] * inverse[0][b]
                    for a in range(1, b + 1):
                        total = total + held[a] * inverse[a][b]
                    out[b, z, rows] = total
            return 0

        lax.fori_loop(c * length, (c + 1) * length, one, 0, unroll=4)
        part = pl.ds(c * length, length)
        stores.append(
            pltpu.make_async_copy(out.at[:, part], result.at[:, part], store_sem.at[c])
        )
        stores[-1].start()
    for store in [*stores, factor_store]:
        store.wait()


def per_device(sizes, ncells, orbitals, potential):
    norb, size_z, size_y, size_x = orbitals.shape
    assert size_x == LANES and size_z % ROWS == 0 and size_y == 2 * ROWS
    assert sizes == (4, 16, 4)
    hbm = pl.BlockSpec(memory_space=pltpu.HBM)
    vmem = pl.BlockSpec(memory_space=pltpu.VMEM)
    f32 = jnp.float32
    groups = size_z // ROWS
    devices = sizes[0] * sizes[1] * sizes[2]
    orbitals = pltpu.with_memory_space_constraint(orbitals, pltpu.HBM)
    potential = pltpu.with_memory_space_constraint(potential, pltpu.HBM)
    filtered, gram = pl.pallas_call(
        functools.partial(filter_kernel, sizes),
        out_shape=(
            jax.ShapeDtypeStruct(orbitals.shape, f32),
            jax.ShapeDtypeStruct((1, LANES), f32),
        ),
        in_specs=[hbm, hbm],
        out_specs=(vmem, vmem),
        scratch_shapes=[
            pltpu.VMEM((DEG, norb, size_z + 2 * REACH, size_y + 2 * ROWS, LANES), f32),
            pltpu.VMEM((size_z, size_y, LANES), f32),
            pltpu.VMEM(orbitals.shape, f32),
            pltpu.VMEM((DEG, size_z, size_y, LANES), f32),
            pltpu.VMEM((DEG, norb, groups, ROWS, LANES), f32),
            pltpu.VMEM((DEG, norb, 2, groups, ROWS, LANES), f32),
            pltpu.VMEM((2 * LANES, LANES), jnp.bfloat16),
            pltpu.VMEM((ROWS * size_y, LANES), jnp.bfloat16),
            pltpu.VMEM((norb * norb, ROWS, LANES), f32),
            pltpu.VMEM((devices, LANES), f32),
            pltpu.SemaphoreType.DMA((norb + 1,)),
            pltpu.SemaphoreType.DMA((DEG, norb, 3)),
            pltpu.SemaphoreType.DMA((DEG, norb, 3)),
            pltpu.SemaphoreType.DMA,
            pltpu.SemaphoreType.DMA,
            pltpu.SemaphoreType.REGULAR,
            pltpu.SemaphoreType.REGULAR,
            pltpu.SemaphoreType.REGULAR,
        ],
        compiler_params=pltpu.CompilerParams(
            collective_id=0, has_side_effects=True, vmem_limit_bytes=32 * 2**20
        ),
        name="filter_and_gram",
    )(orbitals, potential)
    return pl.pallas_call(
        functools.partial(combine_kernel, ncells),
        out_shape=(
            jax.ShapeDtypeStruct(orbitals.shape, f32),
            jax.ShapeDtypeStruct((norb, norb), f32),
        ),
        in_specs=[vmem, vmem],
        out_specs=(hbm, hbm),
        scratch_shapes=[
            pltpu.VMEM(orbitals.shape, f32),
            pltpu.VMEM((norb, norb), f32),
            pltpu.SemaphoreType.DMA((4,)),
            pltpu.SemaphoreType.DMA,
        ],
        compiler_params=pltpu.CompilerParams(vmem_limit_bytes=16 * 2**20),
        name="combine",
    )(gram, filtered)


def solution(mesh):
    sizes = tuple(mesh.shape[a] for a in ("gx", "gy", "gz"))

    def run(orbitals, potential):
        ncells = float(potential.size)
        return jax.shard_map(
            functools.partial(per_device, sizes, ncells),
            mesh=mesh,
            in_specs=(P(None, "gz", "gy", "gx"), P("gz", "gy", "gx")),
            out_specs=(P(None, "gz", "gy", "gx"), P()),
            check_vma=False,
        )(orbitals, potential)

    return run
```
